256 devices in a mesh: mem: 8 (over x_hi, y), grid: 32 (over z, x_lo, core).
Axes of the slice: x: 4 (x_hi: 2, x_lo: 2; x = x_hi * 2 + x_lo), y: 4, z: 8, core: 2. Of those that a mesh axis runs over, the one named last changes fastest.
Arguments:
- ensemble: bfloat16 [1024, 1024, 1024], P(('mem', 'grid')), may hold values from -6 to 6
- right_side: float32 [1024, 1024], P(('mem', 'grid')), may hold values from -18 to 18
- obs_prec: float32 [1024, 1024], P(('mem', 'grid')), may hold values from 0.5 to 2
- neighbors: int32 [1024, 8], replicated, may hold values from 0 to 1023, as said below
- loc_weight: float32 [1024, 8], replicated, may hold values from 0 to 0.08
Outputs:
- solution_field: float32 [1024, 1024], P(('mem', 'grid'))
- residual: float32 [1024, 1024], P(('mem', 'grid'))
The draws below stay inside these ranges and needn't reach their ends.
Inputs may be any that keep to these rules, and one draw needn't show every extreme that they name: neighbors[b, j] lies within 3 of b along the cyclic order of blocks, and every block is listed exactly once in each of the 8 columns.
All inputs are finite; a program needn't handle non-finite values.
Results may differ from the reference program's by a relative error of at most 0.0073.
Values may be sent and summed in bfloat16 or wider, within the bound.
A program may use at most 128 MiB of HBM per device.

```python
import math
import jax
import jax.numpy as jnp
from jax import lax

M = 1024
NB = 8
ITERS = 2
BLK_DEV = 4
CELL = 1024
NBLK = 1024


def draw_right_side(key, part):
    rows = jnp.arange(NBLK, dtype=jnp.float32)[:, None]
    base = jax.random.truncated_normal(key, -6.0, 6.0, (NBLK, CELL), jnp.float32)
    return base * (1.0 + 2.0 * rows / NBLK)


def draw_neighbors(key, part):
    windows = NBLK // BLK_DEV
    columns = []
    for slot in range(NB):
        offset = slot * BLK_DEV // NB
        keys = jax.random.split(jax.random.fold_in(key, slot + 11), windows)
        perms = jax.vmap(lambda k: jax.random.permutation(k, BLK_DEV))(keys).astype(jnp.int32)
        starts = jnp.arange(windows, dtype=jnp.int32)[:, None] * BLK_DEV + offset
        source = (starts + jnp.arange(BLK_DEV, dtype=jnp.int32)[None, :]) % NBLK
        target = (starts + perms) % NBLK
        column = jnp.zeros((NBLK,), jnp.int32).at[source.reshape(-1)].set(target.reshape(-1))
        columns.append(column)
    return jnp.stack(columns, axis=1)


def block_levels(key, shape, shards, low, high):
    factor_of, own = 1.0, jax.random.fold_in(key, 6)
    for position, blocks in shards:
        draws = jnp.exp(jax.random.uniform(jax.random.fold_in(own, position), (blocks,), jnp.float32, low / len(shards), high / len(shards)))
        factor_of = factor_of * jnp.repeat(draws, shape[position] // blocks).reshape([-1 if axis == position else 1 for axis in range(len(shape))])
    return factor_of


def bell_draw(stream_key, dims, scale, limit, cuts=(), held_as=jnp.bfloat16):
    result = jax.random.normal(stream_key, dims, jnp.float32) * scale
    if len(cuts) > 0:
        result = block_levels(stream_key, dims, cuts, -0.22, 0.18) * result
    return jnp.clip(result, min=-limit, max=limit).astype(held_as)


def setup_inputs(seed: int = 0) -> dict:
    splits = jax.random.split(jax.random.key(seed), 6)
    ensemble = bell_draw(splits[0], (M, NBLK, CELL), 1.0, 6.0, ((0, 256),))
    right_side = draw_right_side(jax.random.fold_in(splits[5], 71), 0)
    obs_prec = jnp.clip(0.5 + 1.5 * jax.random.uniform(splits[2], (NBLK, CELL), jnp.float32) ** block_levels(splits[2], (NBLK, CELL), ((0, 256),), -0.2, 0.2), 0.5, 2.0)
    neighbors = draw_neighbors(jax.random.fold_in(splits[5], 71), 0)
    loc_weight = jnp.clip(jax.random.uniform(splits[4], (NBLK, NB), jnp.float32, 0.0, 0.08), 0.0, 0.08)
    return {"ensemble": ensemble, "right_side": right_side, "obs_prec": obs_prec, "neighbors": neighbors, "loc_weight": loc_weight}


def apply_operator(direction, ensemble, obs_prec, neighbors, loc_weight):
    group = math.gcd(NBLK, 32)
    count = NBLK // group
    rounded = direction.astype(jnp.bfloat16)

    def sums_of(k):
        part = lax.dynamic_slice_in_dim(ensemble, k * group, group, 1).astype(jnp.float32)
        dpart = lax.dynamic_slice_in_dim(rounded, k * group, group, 0).astype(jnp.float32)
        return jnp.einsum('mbc,bc->bm', part, dpart)

    block_sum = lax.map(sums_of, jnp.arange(count, dtype=jnp.int32)).reshape(NBLK, M)
    picked = jnp.take(block_sum, neighbors, axis=0)
    coeff = (block_sum + jnp.sum(picked * loc_weight[:, :, None], axis=1)).astype(jnp.bfloat16)

    def spread_of(k):
        part = lax.dynamic_slice_in_dim(ensemble, k * group, group, 1).astype(jnp.float32)
        cpart = lax.dynamic_slice_in_dim(coeff, k * group, group, 0).astype(jnp.float32)
        return jnp.einsum('mbc,bm->bc', part, cpart)

    spread = lax.map(spread_of, jnp.arange(count, dtype=jnp.int32)).reshape(NBLK, CELL)
    return obs_prec * direction + spread * (1.0 / M)


def reference(ensemble, right_side, obs_prec, neighbors, loc_weight):
    solution_field = jnp.zeros_like(right_side)
    residual = right_side
    direction = right_side
    norm_now = jnp.sum(residual * residual)
    for step in range(ITERS):
        image = apply_operator(direction, ensemble, obs_prec, neighbors, loc_weight)
        alpha = norm_now / jnp.sum(direction * image)
        solution_field = solution_field + alpha * direction
        residual = residual - alpha * image
        norm_next = jnp.sum(residual * residual)
        direction = residual + (norm_next / norm_now) * direction
        norm_now = norm_next
    return solution_field, residual
```

```python
import functools

import jax
import jax.numpy as jnp
from jax import lax
from jax.experimental import pallas as pl
from jax.experimental.pallas import tpu as pltpu
from jax.sharding import PartitionSpec as P

M = 1024
ITERS = 2
NX, NY, NZ = 4, 4, 8
LANE = 128
F32, BF16 = jnp.float32, jnp.bfloat16
MESH = pl.DeviceIdType.MESH


def kernel(
    ens, rhs, obs, nbr, wgt, sol_out, res_out,
    half, gath, part, from_r1, line_t, from_r2, line_u, from_r3, whole, from_sib,
    high, low, expand, sums, sums_sib, sums_prev, mix, coeff_t, onehot, select,
    field, stat, stat_in,
    ens_sem, ens_send, ens_recv,
    s0, r0s, s1, r1s, s2, r2s, s3, r3s,
    t1, u1, t2, u2, t3, u3, t4, u4, bs_s, bs_r, st_s, st_r,
):
    mem, grid = lax.axis_index("mem"), lax.axis_index("grid")
    y, z, core = mem % NY, grid // 4, grid % 2
    x = (mem // NY) * 2 + (grid // 2) % 2
    other = 1 - core
    first = core == 0

    def device(xx, yy, zz, cc):
        return ((xx // 2) * NY + yy, zz * 4 + (xx % 2) * 2 + cc)

    sibling = device(x, y, z, other)

    def x_of(d):
        return (x + d) % NX

    def y_of(d):
        return (y + d) % NY

    def z_of(d):
        return (z + d) % NZ

    partners = [sibling]
    partners += [device(x, y, z_of(d), core) for d in range(1, NZ)]
    partners += [device(x_of(d), y, z, core) for d in range(1, NX)]
    partners += [device(x, y_of(d), z, core) for d in range(1, NY)]

    barrier = pltpu.get_barrier_semaphore()
    for there in partners:
        pl.semaphore_signal(barrier, inc=1, device_id=there, device_id_type=MESH)

    def remote(src, dst, send, recv, there):
        return pltpu.make_async_remote_copy(
            src_ref=src, dst_ref=dst, send_sem=send, recv_sem=recv,
            device_id=there, device_id_type=MESH,
        )

    res, direc, prec, answer = (field.at[i] for i in range(4))
    for g in range(8):
        cols = pl.ds(g * LANE, LANE)
        res[pl.ds(4 * g, 4), :] = rhs[:, cols]
        prec[pl.ds(4 * g, 4), :] = obs[:, cols]
    direc[...] = jnp.zeros_like(direc)
    answer[...] = jnp.zeros_like(answer)
    sums_prev[...] = jnp.zeros_like(sums_prev)

    lanes = lax.broadcasted_iota(jnp.int32, (8, M), 1)
    rows = lax.broadcasted_iota(jnp.int32, (8, M), 0)
    onehot[...] = jnp.where(lanes // LANE == rows, 1.0, 0.0).astype(BF16)
    big_lane = lax.broadcasted_iota(jnp.int32, (LANE, M), 1)
    big_row = lax.broadcasted_iota(jnp.int32, (LANE, M), 0)
    select[...] = jnp.where(big_lane // LANE == big_row, 1.0, 0.0).astype(BF16)
    coeff_t[...] = jnp.zeros_like(coeff_t)

    upper = lax.broadcasted_iota(jnp.int32, (8, LANE), 0) < 4

    def total(v):
        return jnp.broadcast_to(jnp.sum(v, axis=(0, 1), keepdims=True), (8, LANE))

    def line(ref, it, xx, yy):
        return ref.at[it, xx // 2, yy, :, xx % 2]

    own_rows = pl.ds(pl.multiple_of(core * 16, 16), 16)
    sib_rows = pl.ds(pl.multiple_of(other * 16, 16), 16)

    pl.semaphore_wait(barrier, len(partners))

    def members(k):
        mine = ens.at[k, :, pl.ds(pl.multiple_of(core * 512, 512), 512)]
        theirs = ens.at[k, :, pl.ds(pl.multiple_of(other * 512, 512), 512)]
        slot = half.at[core * 4 + k]
        return (
            pltpu.make_async_copy(mine, slot, ens_sem.at[k]),
            remote(theirs, slot, ens_send.at[k], ens_recv.at[k], sibling),
        )

    def iteration(it, rr_prev):
        held = []

        def send(*args):
            copy = remote(*args)
            copy.start()
            held.append(copy)
            return copy

        def exchange(kind, value, theres):
            stat[it, kind] = value
            copies = [
                send(stat.at[it, kind], stat_in.at[it, kind, i], st_s.at[it, kind, i], st_r.at[it, kind, i], there)
                for i, there in enumerate(theres)
            ]

            def finish():
                out = value
                for i, copy in enumerate(copies):
                    copy.wait_recv()
                for i in range(len(copies)):
                    out = out + stat_in[it, kind, i]
                return out

            return finish

        z_line = [device(x, y, z_of(d), core) for d in range(1, NZ)]
        x_line = [device(x_of(d), y, z, core) for d in range(1, NX)]
        y_line = [device(x, y_of(d), z, core) for d in range(1, NY)]

        packed = field.at[4 + it]
        r = res[...]
        packed_b = whole.at[it]
        packed_b[...] = r.astype(BF16)
        mine = gath.at[it, x // 2, y, z, x % 2]
        c0 = send(packed_b.at[sib_rows], mine.at[own_rows], s0.at[it], r0s.at[it], sibling)
        rr_fin = exchange(0, total(r * r), [sibling])
        mine[own_rows, :] = packed_b[own_rows, :]
        c0.wait_recv()

        c1 = [
            send(mine, mine, s1.at[it, i], r1s.at[it, i], there)
            for i, there in enumerate(z_line)
        ]
        rr_fin = exchange(1, rr_fin(), z_line)
        return_first = None

        @pl.when(it == 0)
        def _():
            for k in range(4):
                for copy in members(k):
                    copy.start()
            rel = nbr[...] - lanes + 3
            rel = jnp.where(rel < 0, rel + M, rel)
            rel = jnp.where(rel >= M, rel - M, rel)
            w = wgt[...]
            for o in range(7):
                row = jnp.sum(jnp.where(rel == o, w, 0.0), axis=0, keepdims=True)
                mix[pl.ds(o, 1), :] = row + (1.0 if o == 3 else 0.0)

        for copy in c1:
            copy.wait_recv()

        own_line = line(gath, it, x, y)
        c2 = [
            send(own_line, own_line, s2.at[it, i], r2s.at[it, i], there)
            for i, there in enumerate(x_line + y_line)
        ]
        rr_fin = exchange(2, rr_fin(), x_line)

        def hop3(a, b):
            sx = jnp.where(first, x_of(a), x)
            sy = jnp.where(first, y, y_of(b))
            there = device(jnp.where(first, x, x_of(a)), jnp.where(first, y_of(b), y), z, core)
            part_line = line(gath, it, sx, sy)
            return remote(part_line, part_line, s3.at[it, a - 1, b - 1], r3s.at[it, a - 1, b - 1], there)

        for i in range(3):
            c2[i].wait_recv()
        for i in range(3):
            c2[3 + i].wait_recv()
        for b in range(1, 4):
            for a in range(1, 4):
                copy = hop3(a, b)
                copy.start()
                held.append(copy)
        rr_fin = exchange(3, rr_fin(), y_line)

        @pl.when(it == 0)
        def _():
            for k in range(4):
                local, away = members(k)
                local.wait()
                away.wait()

        def block_sums(step):
            yy = y_of(4 - step)

            def body(i, carry):
                xh, zz = i // NZ, i % NZ
                row0 = pl.multiple_of(((xh * NY + yy) * NZ + zz) * 16, 16)
                tiles = [[], [], [], []]
                for xl in range(2):
                    ch = gath[it, xh, yy, zz, xl].astype(F32)
                    for j in range(2):
                        a = ch[8 * j : 8 * j + 8]
                        b = ch[16 + 8 * j : 24 + 8 * j]
                        tiles[2 * j].append(jnp.where(upper, a, pltpu.roll(b, 4, 0)))
                        tiles[2 * j + 1].append(jnp.where(upper, pltpu.roll(a, 4, 0), b))
                tiles = [jnp.concatenate(t, axis=0) for t in tiles]
                at = pl.ds(pl.multiple_of(i * 16, 16), 16)
                for k in range(8):
                    e = half[k, pl.ds(row0, 16), :].astype(F32)
                    acc = e[:, 0:LANE] * tiles[0]
                    for g in range(1, 4):
                        acc = acc + e[:, g * LANE : (g + 1) * LANE] * tiles[g]
                    top = acc.astype(BF16)
                    high[at, k * LANE : (k + 1) * LANE] = top
                    low[at, k * LANE : (k + 1) * LANE] = (acc - top.astype(F32)).astype(BF16)
                return carry

            lax.fori_loop(0, 2 * NZ, body, 0)
            dims = (((1,), (1,)), ((), ()))
            for xh in range(2):
                at = pl.ds(xh * LANE, LANE)
                got = lax.dot_general(onehot[...], high[at, :], dims, preferred_element_type=F32)
                got = got + lax.dot_general(onehot[...], low[at, :], dims, preferred_element_type=F32)
                sums[it, xh * NY + yy] = got
                unit = xh * NY + yy
                copy = remote(
                    sums.at[it, unit], sums_sib.at[it, unit],
                    bs_s.at[it, step, xh], bs_r.at[it, step, xh], sibling,
                )
                copy.start()
                held.append(copy)

        sum_copies = len(held)
        block_sums(0)
        for step in range(1, 4):
            b = jnp.where(first, step, 4 - step)
            for a in range(1, 4):
                dummy = line(gath, it, x, y)
                remote(dummy, dummy, s3.at[it, a - 1, b - 1], r3s.at[it, a - 1, b - 1], sibling).wait_recv()
            block_sums(step)
        sum_copies = held[sum_copies:]

        rr = rr_fin()
        beta = jnp.where(it == 0, 0.0, rr / rr_prev)
        p = r + beta[0:1] * direc[...]
        direc[...] = p
        dp = prec[...] * p
        pdp_fin = exchange(4, total(p * dp), [sibling])
        for copy in sum_copies:
            copy.wait_recv()

        bs = [sums[it, u] + sums_sib[it, u] + beta * sums_prev[u] for u in range(8)]
        for u in range(8):
            sums_prev[u] = bs[u]
        bs = jnp.concatenate(bs, axis=1)
        co = mix[3:4, :] * bs
        for o in (0, 1, 2, 4, 5, 6):
            co = co + mix[o : o + 1, :] * pltpu.roll(bs, (3 - o) % M, 1)
        co = co.astype(BF16).astype(F32)
        quad_fin = exchange(5, total(co * bs) * (1.0 / M) + pdp_fin(), y_line)
        for u in range(8):
            coeff_t[u, 0:8, :] = co[:, u * LANE : (u + 1) * LANE]

        def spread(step):
            yy = y_of(4 - step)
            for xh in range(2):
                cols = coeff_t[xh * NY + yy].T.astype(BF16)
                expand[xh] = jnp.dot(cols, select[...], preferred_element_type=F32)

            def body(i, carry):
                xh, zz = i // NZ, i % NZ
                row0 = pl.multiple_of(((xh * NY + yy) * NZ + zz) * 16, 16)
                at = pl.ds(pl.multiple_of(zz * 16, 16), 16)
                acc = [None] * 4
                for k in range(8):
                    e = half[k, pl.ds(row0, 16), :].astype(F32)
                    ck = expand[xh, at, k * LANE : (k + 1) * LANE]
                    for g in range(4):
                        term = e[:, g * LANE : (g + 1) * LANE] * ck
                        acc[g] = term if k == 0 else acc[g] + term
                for xl in range(2):
                    t = [v[8 * xl : 8 * xl + 8] for v in acc]
                    lo = [jnp.where(upper, t[2 * j], pltpu.roll(t[2 * j + 1], 4, 0)) for j in range(2)]
                    hi = [jnp.where(upper, pltpu.roll(t[2 * j], 4, 0), t[2 * j + 1]) for j in range(2)]
                    part[it, xh, yy, zz, xl] = jnp.concatenate(lo + hi, axis=0).astype(BF16)
                return carry

            lax.fori_loop(0, 2 * NZ, body, 0)

        def hop_r1(p_, q):
            lx = jnp.where(first, x_of(q), x_of(p_))
            ly = jnp.where(first, y_of(p_), y_of(q))
            there = device(jnp.where(first, x, x_of(p_)), jnp.where(first, y_of(p_), y), z, core)
            return remote(line(part, it, lx, ly), from_r1.at[it, p_ - 1, q], t1.at[it, p_ - 1, q], u1.at[it, p_ - 1, q], there)

        for step in (1, 2, 3, 0):
            spread(step)
            if step:

                @pl.when(first)
                def _():
                    for q in range(4):
                        hop_r1(4 - step, q).start()

            @pl.when(jnp.logical_not(first))
            def _():
                for p_ in range(1, 4):
                    hop_r1(p_, (4 - step) % 4).start()

        quad_fin = exchange(6, quad_fin(), x_line)

        def own(q):
            return jnp.where(first, x_of(q), x), jnp.where(first, y, y_of(q))

        c5 = []
        for q in (2, 1, 3, 0):
            for p_ in range(1, 4):
                hop_r1(p_, q).wait_recv()
            lx, ly = own(q)

            def add1(zz, carry, q=q, lx=lx, ly=ly):
                v = part[it, lx // 2, ly, zz, lx % 2].astype(F32)
                for p_ in range(3):
                    v = v + from_r1[it, p_, q, zz].astype(F32)
                if q:
                    line_t[it, q - 1, zz] = v.astype(BF16)
                else:
                    line_u[it, zz] = v
                return carry

            lax.fori_loop(0, NZ, add1, 0)
            if q:
                c5.append(send(line_t.at[it, q - 1], from_r2.at[it, q - 1], t2.at[it, q - 1], u2.at[it, q - 1], device(lx, ly, z, core)))
        for copy in c5:
            copy.wait_recv()

        def add2(zz, carry):
            v = line_u[it, zz]
            for q in range(3):
                v = v + from_r2[it, q, zz].astype(F32)
            line_u[it, zz] = v
            return carry

        lax.fori_loop(0, NZ, add2, 0)

        c6 = [
            send(line_u.at[it, z_of(d)], from_r3.at[it, d - 1], t3.at[it, d - 1], u3.at[it, d - 1], device(x, y, z_of(d), core))
            for d in (4, 3, 5, 2, 6, 1, 7)
        ]
        quad_fin = exchange(7, quad_fin(), z_line)
        for copy in c6:
            copy.wait_recv()
        v = line_u[it, z]
        for d in range(7):
            v = v + from_r3[it, d]
        chip = field.at[4 + it]
        chip[...] = v
        c7 = send(chip.at[sib_rows], from_sib.at[it, own_rows], t4.at[it], u4.at[it], sibling)
        from_sib[it, own_rows, :] = chip[own_rows, :]
        alpha = (rr / quad_fin())[0:1]
        answer[...] = answer[...] + alpha * p
        c7.wait_recv()
        image = dp + from_sib[it] * (1.0 / M)
        res[...] = r - alpha * image

        for copy in held:
            copy.wait_send()
        for p_ in range(1, 4):
            for q in range(4):
                hop_r1(p_, q).wait_send()
        return rr

    lax.fori_loop(0, ITERS, iteration, jnp.ones((8, LANE), F32))

    for g in range(8):
        cols = pl.ds(g * LANE, LANE)
        sol_out[:, cols] = answer[pl.ds(4 * g, 4), :]
        res_out[:, cols] = res[pl.ds(4 * g, 4), :]


def per_device(ensemble, right_side, obs_prec, neighbors, loc_weight):
    vmem = pl.BlockSpec(memory_space=pltpu.VMEM)
    dma = lambda *n: pltpu.SemaphoreType.DMA(n)
    out = jax.ShapeDtypeStruct(right_side.shape, F32)
    return pl.pallas_call(
        kernel,
        out_shape=(out, out),
        in_specs=[pl.BlockSpec(memory_space=pl.ANY), vmem, vmem, vmem, vmem],
        out_specs=(vmem, vmem),
        scratch_shapes=[
            pltpu.VMEM((8, M, 512), BF16),
            pltpu.VMEM((2, 2, NY, NZ, 2, 32, LANE), BF16),
            pltpu.VMEM((2, 2, NY, NZ, 2, 32, LANE), BF16),
            pltpu.VMEM((2, 3, 4, NZ, 32, LANE), BF16),
            pltpu.VMEM((2, 3, NZ, 32, LANE), BF16),
            pltpu.VMEM((2, 3, NZ, 32, LANE), BF16),
            pltpu.VMEM((2, NZ, 32, LANE), F32),
            pltpu.VMEM((2, 7, 32, LANE), F32),
            pltpu.VMEM((2, 32, LANE), BF16),
            pltpu.VMEM((2, 32, LANE), F32),
            pltpu.VMEM((256, M), BF16),
            pltpu.VMEM((256, M), BF16),
            pltpu.VMEM((2, LANE, M), F32),
            pltpu.VMEM((2, 8, 8, LANE), F32),
            pltpu.VMEM((2, 8, 8, LANE), F32),
            pltpu.VMEM((8, 8, LANE), F32),
            pltpu.VMEM((8, M), F32),
            pltpu.VMEM((8, LANE, LANE), F32),
            pltpu.VMEM((8, M), BF16),
            pltpu.VMEM((LANE, M), BF16),
            pltpu.VMEM((6, 32, LANE), F32),
            pltpu.VMEM((2, 8, 8, LANE), F32),
            pltpu.VMEM((2, 8, 7, 8, LANE), F32),
            dma(4), dma(4), dma(4),
            dma(2), dma(2), dma(2, 7), dma(2, 7), dma(2, 6), dma(2, 6), dma(2, 3, 3), dma(2, 3, 3),
            dma(2, 3, 4), dma(2, 3, 4), dma(2, 3), dma(2, 3), dma(2, 7), dma(2, 7), dma(2), dma(2),
            dma(2, 4, 2), dma(2, 4, 2), dma(2, 8, 7), dma(2, 8, 7),
        ],
        compiler_params=pltpu.CompilerParams(
            collective_id=0, has_side_effects=True, vmem_limit_bytes=56 * 2**20
        ),
    )(ensemble, right_side, obs_prec, neighbors.T, loc_weight.T)


def solution(mesh):
    return jax.shard_map(
        per_device,
        mesh=mesh,
        in_specs=(
            P(("mem", "grid"), None, None),
            P(("mem", "grid"), None),
            P(("mem", "grid"), None),
            P(),
            P(),
        ),
        out_specs=(P(("mem", "grid"), None), P(("mem", "grid"), None)),
        check_vma=False,
    )
```

```python
import functools

import jax
import jax.numpy as jnp
from jax import lax
from jax.experimental import pallas as pl
from jax.experimental.pallas import tpu as pltpu
from jax.sharding import PartitionSpec as P

M = 1024
ITERS = 2
NX, NY, NZ = 4, 4, 8
LANE = 128
F32, BF16 = jnp.float32, jnp.bfloat16
MESH = pl.DeviceIdType.MESH


def kernel(
    ens, rhs, obs, nbr, wgt, out,
    half, gath, part, from_r1, line_t, from_r2, line_u, from_r3, packed, whole,
    high, low, expand, sums, sums_sib, sums_prev, mix, coeff_t, onehot, select,
    field, stat, stat_in, span,
    ens_local, ens_send, ens_recv,
    r1s, r2s, r3s, u1, u2, u3, bs_r, st_r, sends,
):
    mem, grid = lax.axis_index("mem"), lax.axis_index("grid")
    y, z, core = mem % NY, grid // 4, grid % 2
    x = (mem // NY) * 2 + (grid // 2) % 2
    other = 1 - core
    first = core == 0

    def device(xx, yy, zz, cc):
        return ((xx // 2) * NY + yy, zz * 4 + (xx % 2) * 2 + cc)

    sibling = device(x, y, z, other)

    def x_of(d):
        return (x + d) % NX

    def y_of(d):
        return (y + d) % NY

    def z_of(d):
        return (z + d) % NZ

    def fwd(d):
        return device(jnp.where(first, x_of(d), x), jnp.where(first, y, y_of(d)), z, core)

    def cross(d):
        return device(jnp.where(first, x, x_of(d)), jnp.where(first, y_of(d), y), z, core)

    z_steps = [(d, 0) for d in range(1, NZ)] + [(d, 1) for d in range(NZ)]
    z_line = [device(x, y, z_of(d), other if e else core) for d, e in z_steps]
    far_first = sorted(range(15), key=lambda i: -min(z_steps[i][0], NZ - z_steps[i][0]))
    fwd_line = [fwd(d) for d in range(1, 4)]
    cross_line = [cross(d) for d in range(1, 4)]
    partners = z_line + fwd_line + cross_line

    barrier = pltpu.get_barrier_semaphore()
    for there in partners:
        pl.semaphore_signal(barrier, inc=1, device_id=there, device_id_type=MESH)

    def remote(src, dst, send, recv, there):
        return pltpu.make_async_remote_copy(
            src_ref=src, dst_ref=dst, send_sem=send, recv_sem=recv,
            device_id=there, device_id_type=MESH,
        )

    res, direc, prec, answer = (field.at[i] for i in range(4))
    for g in range(8):
        cols = pl.ds(g * LANE, LANE)
        res[pl.ds(4 * g, 4), :] = rhs[:, cols]
        prec[pl.ds(4 * g, 4), :] = obs[:, cols]
    direc[...] = jnp.zeros_like(direc)
    answer[...] = jnp.zeros_like(answer)
    sums_prev[...] = jnp.zeros_like(sums_prev)

    lanes = lax.broadcasted_iota(jnp.int32, (8, M), 1)
    rows = lax.broadcasted_iota(jnp.int32, (8, M), 0)
    onehot[...] = jnp.where(lanes // LANE == rows, 1.0, 0.0).astype(BF16)
    big_lane = lax.broadcasted_iota(jnp.int32, (LANE, M), 1)
    big_row = lax.broadcasted_iota(jnp.int32, (LANE, M), 0)
    select[...] = jnp.where(big_lane // LANE == big_row, 1.0, 0.0).astype(BF16)
    coeff_t[...] = jnp.zeros_like(coeff_t)

    upper = lax.broadcasted_iota(jnp.int32, (8, LANE), 0) < 4

    def total(v):
        return jnp.broadcast_to(jnp.sum(v, axis=(0, 1), keepdims=True), (1, LANE))

    def line(ref, it, xx, yy):
        return ref.at[it, xx // 2, yy, :, xx % 2]

    own_rows = pl.ds(pl.multiple_of(core * 16, 16), 16)
    sib_rows = pl.ds(pl.multiple_of(other * 16, 16), 16)
    mine_four = half.at[pl.ds(pl.multiple_of(core * 4, 4), 4)]
    sib_four = half.at[pl.ds(pl.multiple_of(other * 4, 4), 4)]

    def members_local():
        src = ens.at[:, :, pl.ds(pl.multiple_of(core * 512, 512), 512)]
        return pltpu.make_async_copy(src, mine_four, ens_local)

    def members_away():
        src = ens.at[:, :, pl.ds(pl.multiple_of(other * 512, 512), 512)]
        return remote(src, mine_four, ens_send, ens_recv, sibling)

    members_local().start()
    pl.semaphore_wait(barrier, len(partners))

    def wait_bytes(ref, sem):
        pltpu.make_async_copy(ref, ref, sem).wait()

    def iteration(it, rr_prev):
        def send(src, dst, kind, recv, there):
            remote(src, dst, sends.at[kind], recv, there).start()

        def landed(dst, recv):
            pltpu.make_async_copy(dst, dst, recv).wait()

        def exchange(kind, slot, value, theres):
            stat[it, kind] = value
            for i, there in enumerate(theres):
                send(stat.at[it, kind], stat_in.at[it, slot + i], 5, st_r.at[it, kind], there)

            def finish():
                wait_bytes(stat_in.at[it, pl.ds(slot, len(theres))], st_r.at[it, kind])
                got = value
                for i in range(len(theres)):
                    got = got + stat_in[it, slot + i]
                return got

            return finish

        r = res[...]
        pack = packed.at[it]
        pack[...] = r.astype(BF16)
        mine = gath.at[it, x // 2, y, z, x % 2]
        for i in far_first:
            send(pack.at[sib_rows if z_steps[i][1] else own_rows], mine.at[own_rows], 0, r1s.at[it, i], z_line[i])
        rr_fin = exchange(0, 0, total(r * r), z_line)
        mine[own_rows, :] = pack[own_rows, :]

        @pl.when(it == 0)
        def _():
            members_away().start()
            rel = nbr[...] - lanes + 3
            rel = jnp.where(rel < 0, rel + M, rel)
            rel = jnp.where(rel >= M, rel - M, rel)
            w = wgt[...]
            for o in range(7):
                row = jnp.sum(jnp.where(rel == o, w, 0.0), axis=0, keepdims=True)
                mix[pl.ds(o, 1), :] = row + (1.0 if o == 3 else 0.0)

        for i in range(15):
            landed(mine.at[own_rows], r1s.at[it, i])

        own_line = line(gath, it, x, y)
        for d in (2, 1, 3):
            send(own_line, own_line, 1, r2s.at[it, d - 1], fwd(d))
        rr_fin = exchange(1, 15, rr_fin(), fwd_line)
        for d in (2, 1, 3):
            send(own_line, own_line, 1, r2s.at[it, 2 + d], cross(d))

        for n, a in enumerate((1, 3, 2)):
            landed(own_line, r2s.at[it, a - 1])
            came = line(gath, it, jnp.where(first, x_of(NX - a), x), jnp.where(first, y, y_of(NY - a)))
            for b in (1, 3, 2):
                send(came, came, 1, r3s.at[it, a - 1, b - 1], cross(b))
        rr_fin = exchange(2, 18, rr_fin(), cross_line)
        for b in range(3):
            landed(own_line, r2s.at[it, 3 + b])

        @pl.when(it == 0)
        def _():
            members_local().wait()
            wait_bytes(sib_four, ens_recv)

        def block_sums(step):
            yy = y_of(4 - step)

            def body(i, carry):
                xh, zz = i // NZ, i % NZ
                row0 = pl.multiple_of(((xh * NY + yy) * NZ + zz) * 16, 16)
                tiles = [[], [], [], []]
                for xl in range(2):
                    ch = gath[it, xh, yy, zz, xl].astype(F32)
                    for j in range(2):
                        a = ch[8 * j : 8 * j + 8]
                        b = ch[16 + 8 * j : 24 + 8 * j]
                        tiles[2 * j].append(jnp.where(upper, a, pltpu.roll(b, 4, 0)))
                        tiles[2 * j + 1].append(jnp.where(upper, pltpu.roll(a, 4, 0), b))
                tiles = [jnp.concatenate(t, axis=0) for t in tiles]
                at = pl.ds(pl.multiple_of(i * 16, 16), 16)
                for k in range(8):
                    e = half[k, pl.ds(row0, 16), :].astype(F32)
                    acc = e[:, 0:LANE] * tiles[0]
                    for g in range(1, 4):
                        acc = acc + e[:, g * LANE : (g + 1) * LANE] * tiles[g]
                    top = acc.astype(BF16)
                    high[at, k * LANE : (k + 1) * LANE] = top
                    low[at, k * LANE : (k + 1) * LANE] = (acc - top.astype(F32)).astype(BF16)
                return carry

            lax.fori_loop(0, 2 * NZ, body, 0)
            dims = (((1,), (1,)), ((), ()))
            for xh in range(2):
                at = pl.ds(xh * LANE, LANE)
                got = lax.dot_general(onehot[...], high[at, :], dims, preferred_element_type=F32)
                got = got + lax.dot_general(onehot[...], low[at, :], dims, preferred_element_type=F32)
                sums[it, xh * NY + yy] = got
                unit = xh * NY + yy
                send(sums.at[it, unit], sums_sib.at[it, unit], 4, bs_r.at[it], sibling)

        for step in (0, 1, 3, 2):
            if step:
                for i in range(1, 4):
                    a, b = jnp.where(first, i, step), jnp.where(first, step, i)
                    landed(own_line, r3s.at[it, a - 1, b - 1])
            block_sums(step)

        rr = rr_fin()
        beta = jnp.where(it == 0, 0.0, rr / rr_prev)
        p = r + beta * direc[...]
        direc[...] = p
        dp = prec[...] * p
        pdp = total(p * dp)
        wait_bytes(sums_sib.at[it], bs_r.at[it])

        bs = [sums[it, u] + sums_sib[it, u] + beta * sums_prev[u] for u in range(8)]
        for u in range(8):
            sums_prev[u] = bs[u]
        bs = jnp.concatenate(bs, axis=1)
        co = mix[3:4, :] * bs
        for o in (0, 1, 2, 4, 5, 6):
            co = co + mix[o : o + 1, :] * pltpu.roll(bs, (3 - o) % M, 1)
        co = co.astype(BF16).astype(F32)
        quad_fin = exchange(3, 21, total(co * bs) * (0.5 / M) + pdp, cross_line)
        for u in range(8):
            coeff_t[u, 0:8, :] = co[:, u * LANE : (u + 1) * LANE]

        def spread(step):
            yy = y_of(4 - step)
            for xh in range(2):
                cols = coeff_t[xh * NY + yy].T.astype(BF16)
                expand[xh] = jnp.dot(cols, select[...], preferred_element_type=F32)

            def body(i, carry):
                xh, zz = i // NZ, i % NZ
                row0 = pl.multiple_of(((xh * NY + yy) * NZ + zz) * 16, 16)
                at = pl.ds(pl.multiple_of(zz * 16, 16), 16)
                acc = [None] * 4
                for k in range(8):
                    e = half[k, pl.ds(row0, 16), :].astype(F32)
                    ck = expand[xh, at, k * LANE : (k + 1) * LANE]
                    for g in range(4):
                        term = e[:, g * LANE : (g + 1) * LANE] * ck
                        acc[g] = term if k == 0 else acc[g] + term
                for xl in range(2):
                    t = [v[8 * xl : 8 * xl + 8] for v in acc]
                    lo = [jnp.where(upper, t[2 * j], pltpu.roll(t[2 * j + 1], 4, 0)) for j in range(2)]
                    hi = [jnp.where(upper, pltpu.roll(t[2 * j], 4, 0), t[2 * j + 1]) for j in range(2)]
                    part[it, xh, yy, zz, xl] = jnp.concatenate(lo + hi, axis=0).astype(BF16)
                return carry

            lax.fori_loop(0, 2 * NZ, body, 0)

        def hop_r1(p_, q):
            lx = jnp.where(first, x_of(q), x_of(p_))
            ly = jnp.where(first, y_of(p_), y_of(q))
            there = device(jnp.where(first, x, x_of(p_)), jnp.where(first, y_of(p_), y), z, core)
            return remote(line(part, it, lx, ly), from_r1.at[it, p_ - 1, q], sends.at[2], u1.at[it, p_ - 1, q], there)

        for step in (2, 1, 3, 0):
            spread(step)
            if step:

                @pl.when(first)
                def _():
                    for q in (2, 1, 3, 0):
                        hop_r1(4 - step, q).start()

            @pl.when(jnp.logical_not(first))
            def _():
                for p_ in (2, 1, 3):
                    hop_r1(p_, (4 - step) % 4).start()

        quad_fin = exchange(4, 24, quad_fin(), fwd_line)

        def own(q):
            return jnp.where(first, x_of(q), x), jnp.where(first, y, y_of(q))

        for q in (2, 1, 3, 0):
            for p_ in range(1, 4):
                landed(from_r1.at[it, p_ - 1, q], u1.at[it, p_ - 1, q])
            lx, ly = own(q)

            def add1(zz, carry, q=q, lx=lx, ly=ly):
                v = part[it, lx // 2, ly, zz, lx % 2].astype(F32)
                for p_ in range(3):
                    v = v + from_r1[it, p_, q, zz].astype(F32)
                if q:
                    line_t[it, q - 1, zz] = v.astype(BF16)
                else:
                    line_u[it, zz] = v
                return carry

            lax.fori_loop(0, NZ, add1, 0)
            if q:
                send(line_t.at[it, q - 1], from_r2.at[it, q - 1], 2, u2.at[it, q - 1], device(lx, ly, z, core))
        quad_fin = exchange(5, 27, quad_fin(), z_line)
        for q in range(3):
            landed(from_r2.at[it, q], u2.at[it, q])

        def add2(zz, carry):
            v = line_u[it, zz]
            for q in range(3):
                v = v + from_r2[it, q, zz].astype(F32)
            line_u[it, zz] = v
            return carry

        lax.fori_loop(0, NZ, add2, 0)

        for i in far_first:
            d, e = z_steps[i]
            send(line_u.at[it, z_of(d), sib_rows if e else own_rows], from_r3.at[it, i], 3, u3.at[it], z_line[i])
        answer_rr = rr / quad_fin()
        answer[...] = answer[...] + answer_rr * p
        wait_bytes(from_r3.at[it], u3.at[it])
        v = line_u[it, z, own_rows, :]
        for i in range(7):
            v = v + from_r3[it, i]
        whole[own_rows, :] = v
        v = from_r3[it, 7]
        for i in range(8, 15):
            v = v + from_r3[it, i]
        whole[sib_rows, :] = v
        res[...] = r - answer_rr * (dp + whole[...] * (1.0 / M))

        wait_bytes(span.at[0:240], sends.at[0])
        wait_bytes(half.at[0, 0:960], sends.at[1])
        wait_bytes(half.at[0, 0:960], sends.at[2])
        wait_bytes(from_r3.at[it], sends.at[3])
        wait_bytes(sums_sib.at[it], sends.at[4])
        wait_bytes(stat_in.at[it], sends.at[5])
        return rr

    lax.fori_loop(0, ITERS, iteration, jnp.ones((1, LANE), F32))
    wait_bytes(mine_four, ens_send)

    for g in range(8):
        cols = pl.ds(g * LANE, LANE)
        out[0:4, cols] = answer[pl.ds(4 * g, 4), :]
        out[4:8, cols] = res[pl.ds(4 * g, 4), :]


def per_device(ensemble, right_side, obs_prec, neighbors, loc_weight):
    vmem = pl.BlockSpec(memory_space=pltpu.VMEM)
    dma = lambda *n: pltpu.SemaphoreType.DMA(n)
    both = pl.pallas_call(
        kernel,
        out_shape=jax.ShapeDtypeStruct((8, M), F32),
        in_specs=[pl.BlockSpec(memory_space=pl.ANY), vmem, vmem, vmem, vmem],
        out_specs=vmem,
        scratch_shapes=[
            pltpu.VMEM((8, M, 512), BF16),
            pltpu.VMEM((2, 2, NY, NZ, 2, 32, LANE), BF16),
            pltpu.VMEM((2, 2, NY, NZ, 2, 32, LANE), BF16),
            pltpu.VMEM((2, 3, 4, NZ, 32, LANE), BF16),
            pltpu.VMEM((2, 3, NZ, 32, LANE), BF16),
            pltpu.VMEM((2, 3, NZ, 32, LANE), BF16),
            pltpu.VMEM((2, NZ, 32, LANE), F32),
            pltpu.VMEM((2, 15, 16, LANE), F32),
            pltpu.VMEM((2, 32, LANE), BF16),
            pltpu.VMEM((32, LANE), F32),
            pltpu.VMEM((256, M), BF16),
            pltpu.VMEM((256, M), BF16),
            pltpu.VMEM((2, LANE, M), F32),
            pltpu.VMEM((2, 8, 8, LANE), F32),
            pltpu.VMEM((2, 8, 8, LANE), F32),
            pltpu.VMEM((8, 8, LANE), F32),
            pltpu.VMEM((8, M), F32),
            pltpu.VMEM((8, LANE, LANE), F32),
            pltpu.VMEM((8, M), BF16),
            pltpu.VMEM((LANE, M), BF16),
            pltpu.VMEM((4, 32, LANE), F32),
            pltpu.VMEM((2, 6, 1, LANE), F32),
            pltpu.VMEM((2, 42, 1, LANE), F32),
            pltpu.VMEM((240, LANE), BF16),
            pltpu.SemaphoreType.DMA, pltpu.SemaphoreType.DMA, pltpu.SemaphoreType.DMA,
            dma(2, 15), dma(2, 6), dma(2, 3, 3), dma(2, 3, 4), dma(2, 3), dma(2), dma(2), dma(2, 6), dma(6),
        ],
        compiler_params=pltpu.CompilerParams(
            collective_id=0, has_side_effects=True, vmem_limit_bytes=56 * 2**20
        ),
    )(ensemble, right_side, obs_prec, neighbors.T, loc_weight.T)
    return both[:4], both[4:]


def solution(mesh):
    return jax.shard_map(
        per_device,
        mesh=mesh,
        in_specs=(
            P(("mem", "grid"), None, None),
            P(("mem", "grid"), None),
            P(("mem", "grid"), None),
            P(),
            P(),
        ),
        out_specs=(P(("mem", "grid"), None), P(("mem", "grid"), None)),
        check_vma=False,
    )
```

```python
import functools

import jax
import jax.numpy as jnp
from jax import lax
from jax.experimental import pallas as pl
from jax.experimental.pallas import tpu as pltpu
from jax.sharding import PartitionSpec as P

M = 1024
ITERS = 2
NX, NY, NZ = 4, 4, 8
LANE = 128
F32, BF16 = jnp.float32, jnp.bfloat16
MESH = pl.DeviceIdType.MESH


def kernel(
    ens, rhs, obs, nbr, wgt, out,
    half, gath, part, from_r1, line_t, from_r2, line_u, from_r3, packed, whole,
    high, low, expand, sums, sums_sib, sums_prev, mix, coeff_t, onehot, select,
    field, stat, stat_in, span,
    ens_local, ens_send, ens_recv,
    r1s, r2s, r3s, u1, u2, u3, bs_r, st_r, sends,
):
    mem, grid = lax.axis_index("mem"), lax.axis_index("grid")
    y, z, core = mem % NY, grid // 4, grid % 2
    x = (mem // NY) * 2 + (grid // 2) % 2
    other = 1 - core
    first = core == 0

    def device(xx, yy, zz, cc):
        return ((xx // 2) * NY + yy, zz * 4 + (xx % 2) * 2 + cc)

    sibling = device(x, y, z, other)

    def x_of(d):
        return (x + d) % NX

    def y_of(d):
        return (y + d) % NY

    def z_of(d):
        return (z + d) % NZ

    def fwd(d):
        return device(jnp.where(first, x_of(d), x), jnp.where(first, y, y_of(d)), z, core)

    def cross(d):
        return device(jnp.where(first, x, x_of(d)), jnp.where(first, y_of(d), y), z, core)

    z_steps = [(d, 0) for d in range(1, NZ)] + [(d, 1) for d in range(NZ)]
    z_line = [device(x, y, z_of(d), other if e else core) for d, e in z_steps]
    far_first = sorted(range(15), key=lambda i: -min(z_steps[i][0], NZ - z_steps[i][0]))
    fwd_line = [fwd(d) for d in range(1, 4)]
    cross_line = [cross(d) for d in range(1, 4)]
    near = [(1, 1), (1, 3), (3, 1), (3, 3)]

    def diagonal(a, b):
        return device(jnp.where(first, x_of(a), x_of(b)), jnp.where(first, y_of(b), y_of(a)), z, core)

    partners = z_line + fwd_line + cross_line + [diagonal(a, b) for a, b in near]

    barrier = pltpu.get_barrier_semaphore()
    for there in partners:
        pl.semaphore_signal(barrier, inc=1, device_id=there, device_id_type=MESH)

    def remote(src, dst, send, recv, there):
        return pltpu.make_async_remote_copy(
            src_ref=src, dst_ref=dst, send_sem=send, recv_sem=recv,
            device_id=there, device_id_type=MESH,
        )

    res, direc, prec, answer = (field.at[i] for i in range(4))
    for g in range(8):
        cols = pl.ds(g * LANE, LANE)
        res[pl.ds(4 * g, 4), :] = rhs[:, cols]
        prec[pl.ds(4 * g, 4), :] = obs[:, cols]
    direc[...] = jnp.zeros_like(direc)
    answer[...] = jnp.zeros_like(answer)
    sums_prev[...] = jnp.zeros_like(sums_prev)

    lanes = lax.broadcasted_iota(jnp.int32, (8, M), 1)
    rows = lax.broadcasted_iota(jnp.int32, (8, M), 0)
    onehot[...] = jnp.where(lanes // LANE == rows, 1.0, 0.0).astype(BF16)
    big_lane = lax.broadcasted_iota(jnp.int32, (LANE, M), 1)
    big_row = lax.broadcasted_iota(jnp.int32, (LANE, M), 0)
    select[...] = jnp.where(big_lane // LANE == big_row, 1.0, 0.0).astype(BF16)
    coeff_t[...] = jnp.zeros_like(coeff_t)

    upper = lax.broadcasted_iota(jnp.int32, (8, LANE), 0) < 4

    def total(v):
        return jnp.broadcast_to(jnp.sum(v, axis=(0, 1), keepdims=True), (1, LANE))

    def line(ref, it, xx, yy):
        return ref.at[it, xx // 2, yy, :, xx % 2]

    own_rows = pl.ds(pl.multiple_of(core * 16, 16), 16)
    sib_rows = pl.ds(pl.multiple_of(other * 16, 16), 16)
    mine_four = half.at[pl.ds(pl.multiple_of(core * 4, 4), 4)]
    sib_four = half.at[pl.ds(pl.multiple_of(other * 4, 4), 4)]

    def members_local():
        src = ens.at[:, :, pl.ds(pl.multiple_of(core * 512, 512), 512)]
        return pltpu.make_async_copy(src, mine_four, ens_local)

    def members_away():
        src = ens.at[:, :, pl.ds(pl.multiple_of(other * 512, 512), 512)]
        return remote(src, mine_four, ens_send, ens_recv, sibling)

    members_local().start()
    pl.semaphore_wait(barrier, len(partners))

    def wait_bytes(ref, sem):
        pltpu.make_async_copy(ref, ref, sem).wait()

    def iteration(it, rr_prev):
        def send(src, dst, kind, recv, there):
            remote(src, dst, sends.at[kind], recv, there).start()

        def landed(dst, recv):
            pltpu.make_async_copy(dst, dst, recv).wait()

        def exchange(kind, slot, value, theres):
            stat[it, kind] = value
            for i, there in enumerate(theres):
                send(stat.at[it, kind], stat_in.at[it, slot + i], 5, st_r.at[it, kind], there)

            def finish():
                wait_bytes(stat_in.at[it, pl.ds(slot, len(theres))], st_r.at[it, kind])
                got = value
                for i in range(len(theres)):
                    got = got + stat_in[it, slot + i]
                return got

            return finish

        r = res[...]
        pack = packed.at[it]
        pack[...] = r.astype(BF16)
        mine = gath.at[it, x // 2, y, z, x % 2]
        for i in far_first[::-1]:
            send(pack.at[sib_rows if z_steps[i][1] else own_rows], mine.at[own_rows], 0, r1s.at[it, z_steps[i][0]], z_line[i])
        rr_fin = exchange(0, 0, total(r * r), z_line)
        mine[own_rows, :] = pack[own_rows, :]

        @pl.when(it == 0)
        def _():
            members_away().start()
            rel = nbr[...] - lanes + 3
            rel = jnp.where(rel < 0, rel + M, rel)
            rel = jnp.where(rel >= M, rel - M, rel)
            w = wgt[...]
            for o in range(7):
                row = jnp.sum(jnp.where(rel == o, w, 0.0), axis=0, keepdims=True)
                mix[pl.ds(o, 1), :] = row + (1.0 if o == 3 else 0.0)

        own_line = line(gath, it, x, y)
        for d in (0, 1, 7, 2, 6, 3, 5, 4):
            chunk = own_line.at[z_of(NZ - d)]
            landed(chunk if d else chunk.at[sib_rows], r1s.at[it, d])
            for n in (2, 1, 3):
                send(chunk, chunk, 1, r2s.at[it, n - 1], fwd(n))
        rr_fin = exchange(1, 15, rr_fin(), fwd_line)
        for d in (2, 1, 3):
            send(own_line, own_line, 1, r2s.at[it, 2 + d], cross(d))
        for a, b in near:
            send(own_line, own_line, 1, r3s.at[it, jnp.where(first, b, a) - 1], diagonal(a, b))

        rr_fin = exchange(2, 18, rr_fin(), cross_line)
        for a in (1, 3, 2):
            landed(own_line, r2s.at[it, a - 1])
        for i, t in ((2, 1), (2, 3), (1, 2), (3, 2), (2, 2)):
            a, b = jnp.where(first, i, t), jnp.where(first, t, i)
            came = line(gath, it, jnp.where(first, x_of(NX - a), x), jnp.where(first, y, y_of(NY - a)))
            send(came, came, 1, r3s.at[it, t - 1], cross(b))
        for b in range(3):
            landed(own_line, r2s.at[it, 3 + b])

        @pl.when(it == 0)
        def _():
            members_local().wait()
            wait_bytes(sib_four, ens_recv)

        def block_sums(step):
            yy = y_of(4 - step)

            def body(i, carry):
                xh, zz = i // NZ, i % NZ
                row0 = pl.multiple_of(((xh * NY + yy) * NZ + zz) * 16, 16)
                tiles = [[], [], [], []]
                for xl in range(2):
                    ch = gath[it, xh, yy, zz, xl].astype(F32)
                    for j in range(2):
                        a = ch[8 * j : 8 * j + 8]
                        b = ch[16 + 8 * j : 24 + 8 * j]
                        tiles[2 * j].append(jnp.where(upper, a, pltpu.roll(b, 4, 0)))
                        tiles[2 * j + 1].append(jnp.where(upper, pltpu.roll(a, 4, 0), b))
                tiles = [jnp.concatenate(t, axis=0) for t in tiles]
                at = pl.ds(pl.multiple_of(i * 16, 16), 16)
                for k in range(8):
                    e = half[k, pl.ds(row0, 16), :].astype(F32)
                    acc = e[:, 0:LANE] * tiles[0]
                    for g in range(1, 4):
                        acc = acc + e[:, g * LANE : (g + 1) * LANE] * tiles[g]
                    top = acc.astype(BF16)
                    high[at, k * LANE : (k + 1) * LANE] = top
                    low[at, k * LANE : (k + 1) * LANE] = (acc - top.astype(F32)).astype(BF16)
                return carry

            lax.fori_loop(0, 2 * NZ, body, 0)
            dims = (((1,), (1,)), ((), ()))
            for xh in range(2):
                at = pl.ds(xh * LANE, LANE)
                got = lax.dot_general(onehot[...], high[at, :], dims, preferred_element_type=F32)
                got = got + lax.dot_general(onehot[...], low[at, :], dims, preferred_element_type=F32)
                sums[it, xh * NY + yy] = got
                unit = xh * NY + yy
                send(sums.at[it, unit], sums_sib.at[it, unit], 4, bs_r.at[it], sibling)

        for step in (0, 1, 3, 2):
            if step:
                wait_bytes(from_r1.at[it, 0:3], r3s.at[it, step - 1])
            block_sums(step)

        rr = rr_fin()
        beta = jnp.where(it == 0, 0.0, rr / rr_prev)
        p = r + beta * direc[...]
        direc[...] = p
        dp = prec[...] * p
        pdp = total(p * dp)
        wait_bytes(sums_sib.at[it], bs_r.at[it])

        bs = [sums[it, u] + sums_sib[it, u] + beta * sums_prev[u] for u in range(8)]
        for u in range(8):
            sums_prev[u] = bs[u]
        bs = jnp.concatenate(bs, axis=1)
        co = mix[3:4, :] * bs
        for o in (0, 1, 2, 4, 5, 6):
            co = co + mix[o : o + 1, :] * pltpu.roll(bs, (3 - o) % M, 1)
        co = co.astype(BF16).astype(F32)
        quad_fin = exchange(3, 21, total(co * bs) * (0.5 / M) + pdp, cross_line)
        for u in range(8):
            coeff_t[u, 0:8, :] = co[:, u * LANE : (u + 1) * LANE]

        def spread(step, xh):
            yy = y_of(4 - step)
            cols = coeff_t[xh * NY + yy].T.astype(BF16)
            expand[...] = jnp.dot(cols, select[...], preferred_element_type=F32)

            def body(zz, carry):
                row0 = pl.multiple_of(((xh * NY + yy) * NZ + zz) * 16, 16)
                at = pl.ds(pl.multiple_of(zz * 16, 16), 16)
                acc = [None] * 4
                for k in range(8):
                    e = half[k, pl.ds(row0, 16), :].astype(F32)
                    ck = expand[at, k * LANE : (k + 1) * LANE]
                    for g in range(4):
                        term = e[:, g * LANE : (g + 1) * LANE] * ck
                        acc[g] = term if k == 0 else acc[g] + term
                for xl in range(2):
                    t = [v[8 * xl : 8 * xl + 8] for v in acc]
                    lo = [jnp.where(upper, t[2 * j], pltpu.roll(t[2 * j + 1], 4, 0)) for j in range(2)]
                    hi = [jnp.where(upper, pltpu.roll(t[2 * j], 4, 0), t[2 * j + 1]) for j in range(2)]
                    part[it, xh, yy, zz, xl] = jnp.concatenate(lo + hi, axis=0).astype(BF16)
                return carry

            lax.fori_loop(0, NZ, body, 0)

        def line_at(ref, q, p_):
            return line(ref, it, jnp.where(first, x_of(q), x_of(p_)), jnp.where(first, y_of(p_), y_of(q)))

        def hop_r1(q, p_):
            slot = 3 * ((q + 3) % 4) + p_ - 1
            send(line_at(part, q, p_), from_r1.at[it, slot], 2, u1.at[it, 0 if q else 1], cross(p_))

        for step in (2, 1, 3, 0):
            for xh in range(2):
                spread(step, xh)

            if step:

                @pl.when(first)
                def _():
                    for q in (2, 1, 3, 0):
                        hop_r1(q, 4 - step)

            @pl.when(jnp.logical_not(first))
            def _():
                for p_ in (2, 1, 3):
                    hop_r1((4 - step) % 4, p_)

        quad_fin = exchange(4, 24, quad_fin(), fwd_line)

        wait_bytes(from_r1.at[it, 0:9], u1.at[it, 0])

        def add1(i, carry):
            d = jnp.where(i % 2 == 1, 4 - (i + 1) // 2, 4 + i // 2)
            zz = z_of(d)
            for q in (2, 1, 3):
                v = line_at(part, q, 0)[zz].astype(F32)
                for p_ in range(3):
                    v = v + from_r1[it, 3 * (q - 1) + p_, zz].astype(F32)
                line_t[it, q - 1, zz] = v.astype(BF16)
                send(line_t.at[it, q - 1, zz], from_r2.at[it, d, q - 1], 2, u2.at[it, d], fwd(q))
            return carry

        lax.fori_loop(0, NZ, add1, 0)
        quad_fin = exchange(5, 27, quad_fin(), z_line)
        wait_bytes(from_r1.at[it, 9:12], u1.at[it, 1])

        own_part = line(part, it, x, y)
        for d in (4, 3, 5, 2, 6, 1, 7, 0):
            zz = z_of(d)
            wait_bytes(from_r2.at[it, d], u2.at[it, d])
            v = own_part[zz].astype(F32)
            for p_ in range(3):
                v = v + from_r1[it, 9 + p_, zz].astype(F32)
            for q in range(3):
                v = v + from_r2[it, d, q].astype(F32)
            line_u[it, zz] = v
            for i in range(15):
                if z_steps[i][0] == d:
                    rows_ = sib_rows if z_steps[i][1] else own_rows
                    send(line_u.at[it, zz, rows_], from_r3.at[it, i], 3, u3.at[it], z_line[i])
        alpha = rr / quad_fin()
        answer[...] = answer[...] + alpha * p
        wait_bytes(from_r3.at[it], u3.at[it])
        v = line_u[it, z, own_rows, :]
        for i in range(7):
            v = v + from_r3[it, i]
        whole[own_rows, :] = v
        v = from_r3[it, 7]
        for i in range(8, 15):
            v = v + from_r3[it, i]
        whole[sib_rows, :] = v
        res[...] = r - alpha * (dp + whole[...] * (1.0 / M))

        wait_bytes(span.at[0:240], sends.at[0])
        wait_bytes(half.at[0, 0:960], sends.at[1])
        wait_bytes(half.at[0, 0:960], sends.at[2])
        wait_bytes(from_r3.at[it], sends.at[3])
        wait_bytes(sums_sib.at[it], sends.at[4])
        wait_bytes(stat_in.at[it], sends.at[5])
        return rr

    lax.fori_loop(0, ITERS, iteration, jnp.ones((1, LANE), F32))
    wait_bytes(mine_four, ens_send)

    for g in range(8):
        cols = pl.ds(g * LANE, LANE)
        out[0:4, cols] = answer[pl.ds(4 * g, 4), :]
        out[4:8, cols] = res[pl.ds(4 * g, 4), :]


def per_device(ensemble, right_side, obs_prec, neighbors, loc_weight):
    vmem = pl.BlockSpec(memory_space=pltpu.VMEM)
    dma = lambda *n: pltpu.SemaphoreType.DMA(n)
    both = pl.pallas_call(
        kernel,
        out_shape=jax.ShapeDtypeStruct((8, M), F32),
        in_specs=[pl.BlockSpec(memory_space=pl.ANY), vmem, vmem, vmem, vmem],
        out_specs=vmem,
        scratch_shapes=[
            pltpu.VMEM((8, M, 512), BF16),
            pltpu.VMEM((2, 2, NY, NZ, 2, 32, LANE), BF16),
            pltpu.VMEM((2, 2, NY, NZ, 2, 32, LANE), BF16),
            pltpu.VMEM((2, 12, NZ, 32, LANE), BF16),
            pltpu.VMEM((2, 3, NZ, 32, LANE), BF16),
            pltpu.VMEM((2, NZ, 3, 32, LANE), BF16),
            pltpu.VMEM((2, NZ, 32, LANE), F32),
            pltpu.VMEM((2, 15, 16, LANE), F32),
            pltpu.VMEM((2, 32, LANE), BF16),
            pltpu.VMEM((32, LANE), F32),
            pltpu.VMEM((256, M), BF16),
            pltpu.VMEM((256, M), BF16),
            pltpu.VMEM((LANE, M), F32),
            pltpu.VMEM((2, 8, 8, LANE), F32),
            pltpu.VMEM((2, 8, 8, LANE), F32),
            pltpu.VMEM((8, 8, LANE), F32),
            pltpu.VMEM((8, M), F32),
            pltpu.VMEM((8, LANE, LANE), F32),
            pltpu.VMEM((8, M), BF16),
            pltpu.VMEM((LANE, M), BF16),
            pltpu.VMEM((4, 32, LANE), F32),
            pltpu.VMEM((2, 6, 1, LANE), F32),
            pltpu.VMEM((2, 42, 1, LANE), F32),
            pltpu.VMEM((240, LANE), BF16),
            pltpu.SemaphoreType.DMA, pltpu.SemaphoreType.DMA, pltpu.SemaphoreType.DMA,
            dma(2, NZ), dma(2, 6), dma(2, 3), dma(2, 2), dma(2, NZ), dma(2), dma(2), dma(2, 6), dma(6),
        ],
        compiler_params=pltpu.CompilerParams(
            collective_id=0, has_side_effects=True, vmem_limit_bytes=56 * 2**20
        ),
    )(ensemble, right_side, obs_prec, neighbors.T, loc_weight.T)
    return both[:4], both[4:]


def solution(mesh):
    return jax.shard_map(
        per_device,
        mesh=mesh,
        in_specs=(
            P(("mem", "grid"), None, None),
            P(("mem", "grid"), None),
            P(("mem", "grid"), None),
            P(),
            P(),
        ),
        out_specs=(P(("mem", "grid"), None), P(("mem", "grid"), None)),
        check_vma=False,
    )
```

```python
import functools

import jax
import jax.numpy as jnp
from jax import lax
from jax.experimental import pallas as pl
from jax.experimental.pallas import tpu as pltpu
from jax.sharding import PartitionSpec as P

M = 1024
ITERS = 2
NX, NY, NZ = 4, 4, 8
LANE = 128
F32, BF16 = jnp.float32, jnp.bfloat16
MESH = pl.DeviceIdType.MESH


def kernel(
    ens, rhs, obs, nbr, wgt, out,
    half, gath, part, from_r1, line_t, from_r2, line_u, from_r3, packed, whole,
    high, low, expand, sums, sums_sib, sums_prev, mix, coeff_t, onehot, select,
    field, stat, stat_in, span,
    ens_local, ens_send, ens_recv,
    r1s, r2s, r3s, u1, u2, u3, bs_r, st_r, sends,
):
    mem, grid = lax.axis_index("mem"), lax.axis_index("grid")
    y, z, core = mem % NY, grid // 4, grid % 2
    x = (mem // NY) * 2 + (grid // 2) % 2
    other = 1 - core
    first = core == 0

    def device(xx, yy, zz, cc):
        return ((xx // 2) * NY + yy, zz * 4 + (xx % 2) * 2 + cc)

    sibling = device(x, y, z, other)

    def x_of(d):
        return (x + d) % NX

    def y_of(d):
        return (y + d) % NY

    def z_of(d):
        return (z + d) % NZ

    def fwd(d):
        return device(jnp.where(first, x_of(d), x), jnp.where(first, y, y_of(d)), z, core)

    def cross(d):
        return device(jnp.where(first, x, x_of(d)), jnp.where(first, y_of(d), y), z, core)

    z_steps = [(d, 0) for d in range(1, NZ)] + [(d, 1) for d in range(NZ)]
    z_line = [device(x, y, z_of(d), other if e else core) for d, e in z_steps]
    far_first = sorted(range(15), key=lambda i: -min(z_steps[i][0], NZ - z_steps[i][0]))
    fwd_line = [fwd(d) for d in range(1, 4)]
    cross_line = [cross(d) for d in range(1, 4)]
    near = [(1, 1), (1, 3), (3, 1), (3, 3)]

    def diagonal(a, b):
        return device(jnp.where(first, x_of(a), x_of(b)), jnp.where(first, y_of(b), y_of(a)), z, core)

    partners = z_line + fwd_line + cross_line + [diagonal(a, b) for a, b in near]

    barrier = pltpu.get_barrier_semaphore()
    for there in partners:
        pl.semaphore_signal(barrier, inc=1, device_id=there, device_id_type=MESH)

    def remote(src, dst, send, recv, there):
        return pltpu.make_async_remote_copy(
            src_ref=src, dst_ref=dst, send_sem=send, recv_sem=recv,
            device_id=there, device_id_type=MESH,
        )

    res, direc, prec, answer = (field.at[i] for i in range(4))
    for g in range(8):
        cols = pl.ds(g * LANE, LANE)
        res[pl.ds(4 * g, 4), :] = rhs[:, cols]
        prec[pl.ds(4 * g, 4), :] = obs[:, cols]
    direc[...] = jnp.zeros_like(direc)
    answer[...] = jnp.zeros_like(answer)
    sums_prev[...] = jnp.zeros_like(sums_prev)

    lanes = lax.broadcasted_iota(jnp.int32, (8, M), 1)
    rows = lax.broadcasted_iota(jnp.int32, (8, M), 0)
    onehot[...] = jnp.where(lanes // LANE == rows, 1.0, 0.0).astype(BF16)
    big_lane = lax.broadcasted_iota(jnp.int32, (LANE, M), 1)
    big_row = lax.broadcasted_iota(jnp.int32, (LANE, M), 0)
    select[...] = jnp.where(big_lane // LANE == big_row, 1.0, 0.0).astype(BF16)
    coeff_t[...] = jnp.zeros_like(coeff_t)

    upper = lax.broadcasted_iota(jnp.int32, (8, LANE), 0) < 4

    def total(v):
        return jnp.broadcast_to(jnp.sum(v, axis=(0, 1), keepdims=True), (1, LANE))

    def line(ref, it, xx, yy):
        return ref.at[it, xx // 2, yy, :, xx % 2]

    own_rows = pl.ds(pl.multiple_of(core * 16, 16), 16)
    sib_rows = pl.ds(pl.multiple_of(other * 16, 16), 16)
    mine_four = half.at[pl.ds(pl.multiple_of(core * 4, 4), 4)]
    sib_four = half.at[pl.ds(pl.multiple_of(other * 4, 4), 4)]

    def members_local():
        src = ens.at[:, :, pl.ds(pl.multiple_of(core * 512, 512), 512)]
        return pltpu.make_async_copy(src, mine_four, ens_local)

    def members_away():
        src = ens.at[:, :, pl.ds(pl.multiple_of(other * 512, 512), 512)]
        return remote(src, mine_four, ens_send, ens_recv, sibling)

    members_local().start()
    pl.semaphore_wait(barrier, len(partners))

    def wait_bytes(ref, sem):
        pltpu.make_async_copy(ref, ref, sem).wait()

    def iteration(it, rr_prev):
        def send(src, dst, kind, recv, there):
            remote(src, dst, sends.at[kind], recv, there).start()

        def landed(dst, recv):
            pltpu.make_async_copy(dst, dst, recv).wait()

        def exchange(kind, slot, value, theres):
            stat[it, kind] = value
            for i, there in enumerate(theres):
                send(stat.at[it, kind], stat_in.at[it, slot + i], 5, st_r.at[it, kind], there)

            def finish():
                wait_bytes(stat_in.at[it, pl.ds(slot, len(theres))], st_r.at[it, kind])
                got = value
                for i in range(len(theres)):
                    got = got + stat_in[it, slot + i]
                return got

            return finish

        r = res[...]
        pack = packed.at[it]
        pack[...] = r.astype(BF16)
        mine = gath.at[it, x // 2, y, z, x % 2]
        for i in far_first[::-1]:
            send(pack.at[sib_rows if z_steps[i][1] else own_rows], mine.at[own_rows], 0, r1s.at[it, z_steps[i][0]], z_line[i])
        rr_fin = exchange(0, 0, total(r * r), z_line)
        mine[own_rows, :] = pack[own_rows, :]

        @pl.when(it == 0)
        def _():
            members_away().start()
            rel = nbr[...] - lanes + 3
            rel = jnp.where(rel < 0, rel + M, rel)
            rel = jnp.where(rel >= M, rel - M, rel)
            w = wgt[...]
            for o in range(7):
                row = jnp.sum(jnp.where(rel == o, w, 0.0), axis=0, keepdims=True)
                mix[pl.ds(o, 1), :] = row + (1.0 if o == 3 else 0.0)

        own_line = line(gath, it, x, y)
        for d in (0, 1, 7, 2, 6, 3, 5, 4):
            chunk = own_line.at[z_of(NZ - d)]
            landed(chunk if d else chunk.at[sib_rows], r1s.at[it, d])
            for n in (2, 1, 3):
                send(chunk, chunk, 1, r2s.at[it, n - 1], fwd(n))
            if d in (0, 1, 7):
                for n in (2, 1, 3):
                    send(chunk, chunk, 1, r2s.at[it, 2 + n], cross(n))
                for a, b in near:
                    send(chunk, chunk, 1, r3s.at[it, jnp.where(first, b, a) - 1], diagonal(a, b))
        rr_fin = exchange(1, 15, rr_fin(), fwd_line)
        for d in (2, 6, 3, 5, 4):
            chunk = own_line.at[z_of(NZ - d)]
            for n in (2, 1, 3):
                send(chunk, chunk, 1, r2s.at[it, 2 + n], cross(n))
        for d in (2, 6, 3, 5, 4):
            chunk = own_line.at[z_of(NZ - d)]
            for a, b in near:
                send(chunk, chunk, 1, r3s.at[it, jnp.where(first, b, a) - 1], diagonal(a, b))

        rr_fin = exchange(2, 18, rr_fin(), cross_line)
        for a in (1, 3, 2):
            landed(own_line, r2s.at[it, a - 1])
        for i, t in ((2, 1), (2, 3), (1, 2), (3, 2), (2, 2)):
            a, b = jnp.where(first, i, t), jnp.where(first, t, i)
            came = line(gath, it, jnp.where(first, x_of(NX - a), x), jnp.where(first, y, y_of(NY - a)))
            send(came, came, 1, r3s.at[it, t - 1], cross(b))
        for b in range(3):
            landed(own_line, r2s.at[it, 3 + b])

        @pl.when(it == 0)
        def _():
            members_local().wait()
            wait_bytes(sib_four, ens_recv)

        def block_sums(step):
            yy = y_of(4 - step)

            def body(i, carry):
                xh, zz = i // NZ, i % NZ
                row0 = pl.multiple_of(((xh * NY + yy) * NZ + zz) * 16, 16)
                tiles = [[], [], [], []]
                for xl in range(2):
                    ch = gath[it, xh, yy, zz, xl].astype(F32)
                    for j in range(2):
                        a = ch[8 * j : 8 * j + 8]
                        b = ch[16 + 8 * j : 24 + 8 * j]
                        tiles[2 * j].append(jnp.where(upper, a, pltpu.roll(b, 4, 0)))
                        tiles[2 * j + 1].append(jnp.where(upper, pltpu.roll(a, 4, 0), b))
                tiles = [jnp.concatenate(t, axis=0) for t in tiles]
                at = pl.ds(pl.multiple_of(i * 16, 16), 16)
                for k in range(8):
                    e = half[k, pl.ds(row0, 16), :].astype(F32)
                    acc = e[:, 0:LANE] * tiles[0]
                    for g in range(1, 4):
                        acc = acc + e[:, g * LANE : (g + 1) * LANE] * tiles[g]
                    top = acc.astype(BF16)
                    high[at, k * LANE : (k + 1) * LANE] = top
                    low[at, k * LANE : (k + 1) * LANE] = (acc - top.astype(F32)).astype(BF16)
                return carry

            lax.fori_loop(0, 2 * NZ, body, 0)
            dims = (((1,), (1,)), ((), ()))
            for xh in range(2):
                at = pl.ds(xh * LANE, LANE)
                got = lax.dot_general(onehot[...], high[at, :], dims, preferred_element_type=F32)
                got = got + lax.dot_general(onehot[...], low[at, :], dims, preferred_element_type=F32)
                sums[it, xh * NY + yy] = got
                unit = xh * NY + yy
                send(sums.at[it, unit], sums_sib.at[it, unit], 4, bs_r.at[it], sibling)

        for step in (0, 1, 3, 2):
            if step:
                wait_bytes(from_r1.at[it, 0:3], r3s.at[it, step - 1])
            block_sums(step)

        rr = rr_fin()
        beta = jnp.where(it == 0, 0.0, rr / rr_prev)
        p = r + beta * direc[...]
        direc[...] = p
        dp = prec[...] * p
        pdp = total(p * dp)
        wait_bytes(sums_sib.at[it], bs_r.at[it])

        bs = [sums[it, u] + sums_sib[it, u] + beta * sums_prev[u] for u in range(8)]
        for u in range(8):
            sums_prev[u] = bs[u]
        bs = jnp.concatenate(bs, axis=1)
        co = mix[3:4, :] * bs
        for o in (0, 1, 2, 4, 5, 6):
            co = co + mix[o : o + 1, :] * pltpu.roll(bs, (3 - o) % M, 1)
        co = co.astype(BF16).astype(F32)
        quad_fin = exchange(3, 21, total(co * bs) * (0.5 / M) + pdp, cross_line)
        for u in range(8):
            coeff_t[u, 0:8, :] = co[:, u * LANE : (u + 1) * LANE]

        def spread(step, xh):
            yy = y_of(4 - step)
            cols = coeff_t[xh * NY + yy].T.astype(BF16)
            expand[...] = jnp.dot(cols, select[...], preferred_element_type=F32)

            def body(zz, carry):
                row0 = pl.multiple_of(((xh * NY + yy) * NZ + zz) * 16, 16)
                at = pl.ds(pl.multiple_of(zz * 16, 16), 16)
                acc = [None] * 4
                for k in range(8):
                    e = half[k, pl.ds(row0, 16), :].astype(F32)
                    ck = expand[at, k * LANE : (k + 1) * LANE]
                    for g in range(4):
                        term = e[:, g * LANE : (g + 1) * LANE] * ck
                        acc[g] = term if k == 0 else acc[g] + term
                for xl in range(2):
                    t = [v[8 * xl : 8 * xl + 8] for v in acc]
                    lo = [jnp.where(upper, t[2 * j], pltpu.roll(t[2 * j + 1], 4, 0)) for j in range(2)]
                    hi = [jnp.where(upper, pltpu.roll(t[2 * j], 4, 0), t[2 * j + 1]) for j in range(2)]
                    part[it, xh, yy, zz, xl] = jnp.concatenate(lo + hi, axis=0).astype(BF16)
                return carry

            lax.fori_loop(0, NZ, body, 0)

        def line_at(ref, q, p_):
            return line(ref, it, jnp.where(first, x_of(q), x_of(p_)), jnp.where(first, y_of(p_), y_of(q)))

        def hop_r1(q, p_):
            slot = 3 * ((q + 3) % 4) + p_ - 1
            send(line_at(part, q, p_), from_r1.at[it, slot], 2, u1.at[it, 0 if q else 1], cross(p_))

        for step in (2, 1, 3, 0):
            for xh in range(2):
                spread(step, xh)

            if step:

                @pl.when(first)
                def _():
                    for q in (2, 1, 3, 0):
                        hop_r1(q, 4 - step)

            @pl.when(jnp.logical_not(first))
            def _():
                for p_ in (2, 1, 3):
                    hop_r1((4 - step) % 4, p_)

        quad_fin = exchange(4, 24, quad_fin(), fwd_line)

        wait_bytes(from_r1.at[it, 0:9], u1.at[it, 0])

        def add1(i, carry):
            d = jnp.where(i % 2 == 1, 4 - (i + 1) // 2, 4 + i // 2)
            zz = z_of(d)
            for q in (2, 1, 3):
                v = line_at(part, q, 0)[zz].astype(F32)
                for p_ in range(3):
                    v = v + from_r1[it, 3 * (q - 1) + p_, zz].astype(F32)
                line_t[it, q - 1, zz] = v.astype(BF16)
                send(line_t.at[it, q - 1, zz], from_r2.at[it, d, q - 1], 2, u2.at[it, d], fwd(q))
            return carry

        lax.fori_loop(0, NZ, add1, 0)
        quad_fin = exchange(5, 27, quad_fin(), z_line)
        wait_bytes(from_r1.at[it, 9:12], u1.at[it, 1])

        own_part = line(part, it, x, y)
        for d in (4, 3, 5, 2, 6, 1, 7, 0):
            zz = z_of(d)
            wait_bytes(from_r2.at[it, d], u2.at[it, d])
            v = own_part[zz].astype(F32)
            for p_ in range(3):
                v = v + from_r1[it, 9 + p_, zz].astype(F32)
            for q in range(3):
                v = v + from_r2[it, d, q].astype(F32)
            line_u[it, zz] = v
            for i in range(15):
                if z_steps[i][0] == d:
                    rows_ = sib_rows if z_steps[i][1] else own_rows
                    send(line_u.at[it, zz, rows_], from_r3.at[it, i], 3, u3.at[it], z_line[i])
        alpha = rr / quad_fin()
        answer[...] = answer[...] + alpha * p
        wait_bytes(from_r3.at[it], u3.at[it])
        v = line_u[it, z, own_rows, :]
        for i in range(7):
            v = v + from_r3[it, i]
        whole[own_rows, :] = v
        v = from_r3[it, 7]
        for i in range(8, 15):
            v = v + from_r3[it, i]
        whole[sib_rows, :] = v
        res[...] = r - alpha * (dp + whole[...] * (1.0 / M))

        wait_bytes(span.at[0:240], sends.at[0])
        wait_bytes(half.at[0, 0:960], sends.at[1])
        wait_bytes(half.at[0, 0:960], sends.at[2])
        wait_bytes(from_r3.at[it], sends.at[3])
        wait_bytes(sums_sib.at[it], sends.at[4])
        wait_bytes(stat_in.at[it], sends.at[5])
        return rr

    lax.fori_loop(0, ITERS, iteration, jnp.ones((1, LANE), F32))
    wait_bytes(mine_four, ens_send)

    for g in range(8):
        cols = pl.ds(g * LANE, LANE)
        out[0:4, cols] = answer[pl.ds(4 * g, 4), :]
        out[4:8, cols] = res[pl.ds(4 * g, 4), :]


def per_device(ensemble, right_side, obs_prec, neighbors, loc_weight):
    vmem = pl.BlockSpec(memory_space=pltpu.VMEM)
    dma = lambda *n: pltpu.SemaphoreType.DMA(n)
    both = pl.pallas_call(
        kernel,
        out_shape=jax.ShapeDtypeStruct((8, M), F32),
        in_specs=[pl.BlockSpec(memory_space=pl.ANY), vmem, vmem, vmem, vmem],
        out_specs=vmem,
        scratch_shapes=[
            pltpu.VMEM((8, M, 512), BF16),
            pltpu.VMEM((2, 2, NY, NZ, 2, 32, LANE), BF16),
            pltpu.VMEM((2, 2, NY, NZ, 2, 32, LANE), BF16),
            pltpu.VMEM((2, 12, NZ, 32, LANE), BF16),
            pltpu.VMEM((2, 3, NZ, 32, LANE), BF16),
            pltpu.VMEM((2, NZ, 3, 32, LANE), BF16),
            pltpu.VMEM((2, NZ, 32, LANE), F32),
            pltpu.VMEM((2, 15, 16, LANE), F32),
            pltpu.VMEM((2, 32, LANE), BF16),
            pltpu.VMEM((32, LANE), F32),
            pltpu.VMEM((256, M), BF16),
            pltpu.VMEM((256, M), BF16),
            pltpu.VMEM((LANE, M), F32),
            pltpu.VMEM((2, 8, 8, LANE), F32),
            pltpu.VMEM((2, 8, 8, LANE), F32),
            pltpu.VMEM((8, 8, LANE), F32),
            pltpu.VMEM((8, M), F32),
            pltpu.VMEM((8, LANE, LANE), F32),
            pltpu.VMEM((8, M), BF16),
            pltpu.VMEM((LANE, M), BF16),
            pltpu.VMEM((4, 32, LANE), F32),
            pltpu.VMEM((2, 6, 1, LANE), F32),
            pltpu.VMEM((2, 42, 1, LANE), F32),
            pltpu.VMEM((240, LANE), BF16),
            pltpu.SemaphoreType.DMA, pltpu.SemaphoreType.DMA, pltpu.SemaphoreType.DMA,
            dma(2, NZ), dma(2, 6), dma(2, 3), dma(2, 2), dma(2, NZ), dma(2), dma(2), dma(2, 6), dma(6),
        ],
        compiler_params=pltpu.CompilerParams(
            collective_id=0, has_side_effects=True, vmem_limit_bytes=56 * 2**20
        ),
    )(ensemble, right_side, obs_prec, neighbors.T, loc_weight.T)
    return both[:4], both[4:]


def solution(mesh):
    return jax.shard_map(
        per_device,
        mesh=mesh,
        in_specs=(
            P(("mem", "grid"), None, None),
            P(("mem", "grid"), None),
            P(("mem", "grid"), None),
            P(),
            P(),
        ),
        out_specs=(P(("mem", "grid"), None), P(("mem", "grid"), None)),
        check_vma=False,
    )
```

```python
import functools

import jax
import jax.numpy as jnp
from jax import lax
from jax.experimental import pallas as pl
from jax.experimental.pallas import tpu as pltpu
from jax.sharding import PartitionSpec as P

M = 1024
ITERS = 2
NX, NY, NZ = 4, 4, 8
LANE = 128
F32, BF16 = jnp.float32, jnp.bfloat16
MESH = pl.DeviceIdType.MESH


def kernel(
    ens, rhs, obs, nbr, wgt, out,
    half, gath, part, from_r1, line_t, from_r2, line_u, from_r3, packed, whole,
    high, low, expand, sums, sums_sib, sums_prev, mix, coeff_t, onehot, select,
    field, stat, stat_in, span,
    ens_local, ens_send, ens_recv,
    r1s, r2s, r3s, u1, u2, u3, bs_r, st_r, sends,
):
    mem, grid = lax.axis_index("mem"), lax.axis_index("grid")
    y, z, core = mem % NY, grid // 4, grid % 2
    x = (mem // NY) * 2 + (grid // 2) % 2
    other = 1 - core
    first = core == 0

    def device(xx, yy, zz, cc):
        return ((xx // 2) * NY + yy, zz * 4 + (xx % 2) * 2 + cc)

    sibling = device(x, y, z, other)

    def x_of(d):
        return (x + d) % NX

    def y_of(d):
        return (y + d) % NY

    def z_of(d):
        return (z + d) % NZ

    def fwd(d):
        return device(jnp.where(first, x_of(d), x), jnp.where(first, y, y_of(d)), z, core)

    def cross(d):
        return device(jnp.where(first, x, x_of(d)), jnp.where(first, y_of(d), y), z, core)

    z_steps = [(d, 0) for d in range(1, NZ)] + [(d, 1) for d in range(NZ)]
    z_line = [device(x, y, z_of(d), other if e else core) for d, e in z_steps]
    far_first = sorted(range(15), key=lambda i: -min(z_steps[i][0], NZ - z_steps[i][0]))
    fwd_line = [fwd(d) for d in range(1, 4)]
    cross_line = [cross(d) for d in range(1, 4)]
    near = [(1, 1), (1, 3), (3, 1), (3, 3)]

    def diagonal(a, b):
        return device(jnp.where(first, x_of(a), x_of(b)), jnp.where(first, y_of(b), y_of(a)), z, core)

    partners = z_line + fwd_line + cross_line + [diagonal(a, b) for a, b in near]

    barrier = pltpu.get_barrier_semaphore()
    for there in partners:
        pl.semaphore_signal(barrier, inc=1, device_id=there, device_id_type=MESH)

    def remote(src, dst, send, recv, there):
        return pltpu.make_async_remote_copy(
            src_ref=src, dst_ref=dst, send_sem=send, recv_sem=recv,
            device_id=there, device_id_type=MESH,
        )

    res, direc, prec, answer = (field.at[i] for i in range(4))
    for g in range(8):
        cols = pl.ds(g * LANE, LANE)
        res[pl.ds(4 * g, 4), :] = rhs[:, cols]
        prec[pl.ds(4 * g, 4), :] = obs[:, cols]
    direc[...] = jnp.zeros_like(direc)
    answer[...] = jnp.zeros_like(answer)
    sums_prev[...] = jnp.zeros_like(sums_prev)

    lanes = lax.broadcasted_iota(jnp.int32, (8, M), 1)
    rows = lax.broadcasted_iota(jnp.int32, (8, M), 0)
    onehot[...] = jnp.where(lanes // LANE == rows, 1.0, 0.0).astype(BF16)
    big_lane = lax.broadcasted_iota(jnp.int32, (LANE, M), 1)
    big_row = lax.broadcasted_iota(jnp.int32, (LANE, M), 0)
    select[...] = jnp.where(big_lane // LANE == big_row, 1.0, 0.0).astype(BF16)
    coeff_t[...] = jnp.zeros_like(coeff_t)

    upper = lax.broadcasted_iota(jnp.int32, (8, LANE), 0) < 4

    def total(v):
        return jnp.broadcast_to(jnp.sum(v, axis=(0, 1), keepdims=True), (1, LANE))

    def line(ref, it, xx, yy):
        return ref.at[it, xx // 2, yy, :, xx % 2]

    own_rows = pl.ds(pl.multiple_of(core * 16, 16), 16)
    sib_rows = pl.ds(pl.multiple_of(other * 16, 16), 16)
    mine_four = half.at[pl.ds(pl.multiple_of(core * 4, 4), 4)]
    sib_four = half.at[pl.ds(pl.multiple_of(other * 4, 4), 4)]

    def members_local():
        src = ens.at[:, :, pl.ds(pl.multiple_of(core * 512, 512), 512)]
        return pltpu.make_async_copy(src, mine_four, ens_local)

    def members_away():
        src = ens.at[:, :, pl.ds(pl.multiple_of(other * 512, 512), 512)]
        return remote(src, mine_four, ens_send, ens_recv, sibling)

    members_local().start()
    pl.semaphore_wait(barrier, len(partners))

    def wait_bytes(ref, sem):
        pltpu.make_async_copy(ref, ref, sem).wait()

    def iteration(it, rr_prev):
        def send(src, dst, kind, recv, there):
            remote(src, dst, sends.at[kind], recv, there).start()

        def landed(dst, recv):
            pltpu.make_async_copy(dst, dst, recv).wait()

        def exchange(kind, slot, value, theres):
            stat[it, kind] = value
            for i, there in enumerate(theres):
                send(stat.at[it, kind], stat_in.at[it, slot + i], 5, st_r.at[it, kind], there)

            def finish():
                wait_bytes(stat_in.at[it, pl.ds(slot, len(theres))], st_r.at[it, kind])
                got = value
                for i in range(len(theres)):
                    got = got + stat_in[it, slot + i]
                return got

            return finish

        r = res[...]
        pack = packed.at[it]
        pack[...] = r.astype(BF16)
        mine = gath.at[it, x // 2, y, z, x % 2]
        for i in far_first[::-1]:
            send(pack.at[sib_rows if z_steps[i][1] else own_rows], mine.at[own_rows], 0, r1s.at[it, z_steps[i][0]], z_line[i])
        rr_fin = exchange(0, 0, total(r * r), z_line)
        mine[own_rows, :] = pack[own_rows, :]

        @pl.when(it == 0)
        def _():
            members_away().start()
            rel = nbr[...] - lanes + 3
            rel = jnp.where(rel < 0, rel + M, rel)
            rel = jnp.where(rel >= M, rel - M, rel)
            w = wgt[...]
            for o in range(7):
                row = jnp.sum(jnp.where(rel == o, w, 0.0), axis=0, keepdims=True)
                mix[pl.ds(o, 1), :] = row + (1.0 if o == 3 else 0.0)

        own_line = line(gath, it, x, y)
        for d in (0, 1, 7, 2, 6, 3, 5, 4):
            chunk = own_line.at[z_of(NZ - d)]
            landed(chunk if d else chunk.at[sib_rows], r1s.at[it, d])
            for n in (2, 1, 3):
                send(chunk, chunk, 1, r2s.at[it, n - 1], fwd(n))
            if d in (0, 1, 7):
                for n in (2, 1, 3):
                    send(chunk, chunk, 1, r2s.at[it, 2 + n], cross(n))
                for a, b in near:
                    send(chunk, chunk, 1, r3s.at[it, jnp.where(first, b, a) - 1], diagonal(a, b))
        rr_fin = exchange(1, 15, rr_fin(), fwd_line)
        for d in (2, 6, 3, 5, 4):
            chunk = own_line.at[z_of(NZ - d)]
            for n in (2, 1, 3):
                send(chunk, chunk, 1, r2s.at[it, 2 + n], cross(n))
        for d in (2, 6, 3, 5, 4):
            chunk = own_line.at[z_of(NZ - d)]
            for a, b in near:
                send(chunk, chunk, 1, r3s.at[it, jnp.where(first, b, a) - 1], diagonal(a, b))

        for a in (1, 3, 2):
            landed(own_line, r2s.at[it, a - 1])
        for i, t in ((2, 1), (2, 3), (1, 2), (3, 2), (2, 2)):
            a, b = jnp.where(first, i, t), jnp.where(first, t, i)
            came = line(gath, it, jnp.where(first, x_of(NX - a), x), jnp.where(first, y, y_of(NY - a)))
            send(came, came, 1, r3s.at[it, t - 1], cross(b))
        rr_fin = exchange(2, 18, rr_fin(), cross_line)
        for b in range(3):
            landed(own_line, r2s.at[it, 3 + b])

        @pl.when(it == 0)
        def _():
            members_local().wait()
            wait_bytes(sib_four, ens_recv)

        def block_sums(step):
            yy = y_of(4 - step)

            def body(i, carry):
                xh, zz = i // NZ, i % NZ
                row0 = pl.multiple_of(((xh * NY + yy) * NZ + zz) * 16, 16)
                tiles = [[], [], [], []]
                for xl in range(2):
                    ch = gath[it, xh, yy, zz, xl].astype(F32)
                    for j in range(2):
                        a = ch[8 * j : 8 * j + 8]
                        b = ch[16 + 8 * j : 24 + 8 * j]
                        tiles[2 * j].append(jnp.where(upper, a, pltpu.roll(b, 4, 0)))
                        tiles[2 * j + 1].append(jnp.where(upper, pltpu.roll(a, 4, 0), b))
                tiles = [jnp.concatenate(t, axis=0) for t in tiles]
                at = pl.ds(pl.multiple_of(i * 16, 16), 16)
                for k in range(8):
                    e = half[k, pl.ds(row0, 16), :].astype(F32)
                    acc = e[:, 0:LANE] * tiles[0]
                    for g in range(1, 4):
                        acc = acc + e[:, g * LANE : (g + 1) * LANE] * tiles[g]
                    top = acc.astype(BF16)
                    high[at, k * LANE : (k + 1) * LANE] = top
                    low[at, k * LANE : (k + 1) * LANE] = (acc - top.astype(F32)).astype(BF16)
                return carry

            lax.fori_loop(0, 2 * NZ, body, 0)
            dims = (((1,), (1,)), ((), ()))
            for xh in range(2):
                at = pl.ds(xh * LANE, LANE)
                got = lax.dot_general(onehot[...], high[at, :], dims, preferred_element_type=F32)
                got = got + lax.dot_general(onehot[...], low[at, :], dims, preferred_element_type=F32)
                sums[it, xh * NY + yy] = got
                unit = xh * NY + yy
                send(sums.at[it, unit], sums_sib.at[it, unit], 4, bs_r.at[it], sibling)

        for step in (0, 1, 3, 2):
            if step:
                wait_bytes(from_r1.at[it, 0:3], r3s.at[it, step - 1])
            block_sums(step)

        rr = rr_fin()
        beta = jnp.where(it == 0, 0.0, rr / rr_prev)
        p = r + beta * direc[...]
        direc[...] = p
        dp = prec[...] * p
        pdp = total(p * dp)
        wait_bytes(sums_sib.at[it], bs_r.at[it])

        bs = [sums[it, u] + sums_sib[it, u] + beta * sums_prev[u] for u in range(8)]
        for u in range(8):
            sums_prev[u] = bs[u]
        bs = jnp.concatenate(bs, axis=1)
        co = mix[3:4, :] * bs
        for o in (0, 1, 2, 4, 5, 6):
            co = co + mix[o : o + 1, :] * pltpu.roll(bs, (3 - o) % M, 1)
        co = co.astype(BF16).astype(F32)
        quad_fin = exchange(3, 21, total(co * bs) * (0.5 / M) + pdp, cross_line)
        for u in range(8):
            coeff_t[u, 0:8, :] = co[:, u * LANE : (u + 1) * LANE]

        def spread(step, xh):
            yy = y_of(4 - step)
            cols = coeff_t[xh * NY + yy].T.astype(BF16)
            expand[...] = jnp.dot(cols, select[...], preferred_element_type=F32)

            def body(zz, carry):
                row0 = pl.multiple_of(((xh * NY + yy) * NZ + zz) * 16, 16)
                at = pl.ds(pl.multiple_of(zz * 16, 16), 16)
                acc = [None] * 4
                for k in range(8):
                    e = half[k, pl.ds(row0, 16), :].astype(F32)
                    ck = expand[at, k * LANE : (k + 1) * LANE]
                    for g in range(4):
                        term = e[:, g * LANE : (g + 1) * LANE] * ck
                        acc[g] = term if k == 0 else acc[g] + term
                for xl in range(2):
                    t = [v[8 * xl : 8 * xl + 8] for v in acc]
                    lo = [jnp.where(upper, t[2 * j], pltpu.roll(t[2 * j + 1], 4, 0)) for j in range(2)]
                    hi = [jnp.where(upper, pltpu.roll(t[2 * j], 4, 0), t[2 * j + 1]) for j in range(2)]
                    part[it, xh, yy, zz, xl] = jnp.concatenate(lo + hi, axis=0).astype(BF16)
                return carry

            lax.fori_loop(0, NZ, body, 0)

        def line_at(ref, q, p_):
            return line(ref, it, jnp.where(first, x_of(q), x_of(p_)), jnp.where(first, y_of(p_), y_of(q)))

        def hop_r1(q, p_):
            slot = 3 * ((q + 3) % 4) + p_ - 1
            send(line_at(part, q, p_), from_r1.at[it, slot], 2, u1.at[it, 0 if q else 1], cross(p_))

        for step in (2, 1, 3, 0):
            for xh in range(2):
                spread(step, xh)

            if step:

                @pl.when(first)
                def _():
                    for q in (2, 1, 3, 0):
                        hop_r1(q, 4 - step)

            @pl.when(jnp.logical_not(first))
            def _():
                for p_ in (2, 1, 3):
                    hop_r1((4 - step) % 4, p_)

        quad_fin = exchange(4, 24, quad_fin(), fwd_line)

        wait_bytes(from_r1.at[it, 0:9], u1.at[it, 0])

        def add1(i, carry):
            d = jnp.where(i % 2 == 1, 4 - (i + 1) // 2, 4 + i // 2)
            zz = z_of(d)
            for q in (2, 1, 3):
                v = line_at(part, q, 0)[zz].astype(F32)
                for p_ in range(3):
                    v = v + from_r1[it, 3 * (q - 1) + p_, zz].astype(F32)
                line_t[it, q - 1, zz] = v.astype(BF16)
                send(line_t.at[it, q - 1, zz], from_r2.at[it, d, q - 1], 2, u2.at[it, d], fwd(q))
            return carry

        lax.fori_loop(0, NZ, add1, 0)
        quad_fin = exchange(5, 27, quad_fin(), z_line)
        wait_bytes(from_r1.at[it, 9:12], u1.at[it, 1])

        own_part = line(part, it, x, y)
        for d in (4, 3, 5, 2, 6, 1, 7, 0):
            zz = z_of(d)
            wait_bytes(from_r2.at[it, d], u2.at[it, d])
            v = own_part[zz].astype(F32)
            for p_ in range(3):
                v = v + from_r1[it, 9 + p_, zz].astype(F32)
            for q in range(3):
                v = v + from_r2[it, d, q].astype(F32)
            line_u[it, zz] = v
            for i in range(15):
                if z_steps[i][0] == d:
                    rows_ = sib_rows if z_steps[i][1] else own_rows
                    send(line_u.at[it, zz, rows_], from_r3.at[it, i], 3, u3.at[it], z_line[i])
        alpha = rr / quad_fin()
        answer[...] = answer[...] + alpha * p
        wait_bytes(from_r3.at[it], u3.at[it])
        v = line_u[it, z, own_rows, :]
        for i in range(7):
            v = v + from_r3[it, i]
        whole[own_rows, :] = v
        v = from_r3[it, 7]
        for i in range(8, 15):
            v = v + from_r3[it, i]
        whole[sib_rows, :] = v
        res[...] = r - alpha * (dp + whole[...] * (1.0 / M))

        wait_bytes(span.at[0:240], sends.at[0])
        wait_bytes(half.at[0, 0:960], sends.at[1])
        wait_bytes(half.at[0, 0:960], sends.at[2])
        wait_bytes(from_r3.at[it], sends.at[3])
        wait_bytes(sums_sib.at[it], sends.at[4])
        wait_bytes(stat_in.at[it], sends.at[5])
        return rr

    lax.fori_loop(0, ITERS, iteration, jnp.ones((1, LANE), F32))
    wait_bytes(mine_four, ens_send)

    for g in range(8):
        cols = pl.ds(g * LANE, LANE)
        out[0:4, cols] = answer[pl.ds(4 * g, 4), :]
        out[4:8, cols] = res[pl.ds(4 * g, 4), :]


def per_device(ensemble, right_side, obs_prec, neighbors, loc_weight):
    vmem = pl.BlockSpec(memory_space=pltpu.VMEM)
    dma = lambda *n: pltpu.SemaphoreType.DMA(n)
    both = pl.pallas_call(
        kernel,
        out_shape=jax.ShapeDtypeStruct((8, M), F32),
        in_specs=[pl.BlockSpec(memory_space=pl.ANY), vmem, vmem, vmem, vmem],
        out_specs=vmem,
        scratch_shapes=[
            pltpu.VMEM((8, M, 512), BF16),
            pltpu.VMEM((2, 2, NY, NZ, 2, 32, LANE), BF16),
            pltpu.VMEM((2, 2, NY, NZ, 2, 32, LANE), BF16),
            pltpu.VMEM((2, 12, NZ, 32, LANE), BF16),
            pltpu.VMEM((2, 3, NZ, 32, LANE), BF16),
            pltpu.VMEM((2, NZ, 3, 32, LANE), BF16),
            pltpu.VMEM((2, NZ, 32, LANE), F32),
            pltpu.VMEM((2, 15, 16, LANE), F32),
            pltpu.VMEM((2, 32, LANE), BF16),
            pltpu.VMEM((32, LANE), F32),
            pltpu.VMEM((256, M), BF16),
            pltpu.VMEM((256, M), BF16),
            pltpu.VMEM((LANE, M), F32),
            pltpu.VMEM((2, 8, 8, LANE), F32),
            pltpu.VMEM((2, 8, 8, LANE), F32),
            pltpu.VMEM((8, 8, LANE), F32),
            pltpu.VMEM((8, M), F32),
            pltpu.VMEM((8, LANE, LANE), F32),
            pltpu.VMEM((8, M), BF16),
            pltpu.VMEM((LANE, M), BF16),
            pltpu.VMEM((4, 32, LANE), F32),
            pltpu.VMEM((2, 6, 1, LANE), F32),
            pltpu.VMEM((2, 42, 1, LANE), F32),
            pltpu.VMEM((240, LANE), BF16),
            pltpu.SemaphoreType.DMA, pltpu.SemaphoreType.DMA, pltpu.SemaphoreType.DMA,
            dma(2, NZ), dma(2, 6), dma(2, 3), dma(2, 2), dma(2, NZ), dma(2), dma(2), dma(2, 6), dma(6),
        ],
        compiler_params=pltpu.CompilerParams(
            collective_id=0, has_side_effects=True, vmem_limit_bytes=56 * 2**20
        ),
    )(ensemble, right_side, obs_prec, neighbors.T, loc_weight.T)
    return both[:4], both[4:]


def solution(mesh):
    return jax.shard_map(
        per_device,
        mesh=mesh,
        in_specs=(
            P(("mem", "grid"), None, None),
            P(("mem", "grid"), None),
            P(("mem", "grid"), None),
            P(),
            P(),
        ),
        out_specs=(P(("mem", "grid"), None), P(("mem", "grid"), None)),
        check_vma=False,
    )
```
